512 devices in a mesh: row: 32 (over z_lo, x), col: 16 (over y, z_hi, core).
Axes of the slice: x: 4, y: 4, z: 16 (z_hi: 2, z_lo: 8; z = z_hi * 8 + z_lo), core: 2. Of those that a mesh axis runs over, the one named last changes fastest.
Arguments:
- anchors: float32 [4096, 4096], P(('row', 'col')), may hold values from 0.2 to 5
- destinations: float32 [4096, 4096], P(('row', 'col')), may hold values from 0.2 to 5
- dest_balance: float32 [4096, 4096], P(('row', 'col')), may hold values from 0.5 to 2
- kernel_hat: float32 [2, 8192, 8192], P(None, ('row', 'col')), as said below
Outputs:
- anchor_balance: float32 [4096, 4096], P(('row', 'col'))
- dest_balance_new: float32 [4096, 4096], P(('row', 'col'))
The draws below stay inside these ranges and needn't reach their ends.
Inputs may be any that keep to these rules, and one draw needn't show every extreme that they name: kernel_hat[0, b, a] and kernel_hat[1, b, a] are the real and imaginary parts of F(kernel)[a, b] for a table kernel of 8192 x 8192 entries, indexed by a row offset and a column offset taken modulo 8192, that is zero on row 4096 and on column 4096 and positive everywhere else.
All inputs are finite; a program needn't handle non-finite values.
Results may differ from the reference program's by a relative error of at most 0.000072.
Values sent between devices are 32-bit elements; how exact they have to be, the bound alone decides.
A program may use at most 64 MiB of HBM per device.

```python
import math
import jax
import jax.numpy as jnp
from jax import lax

N = 4096
P_SIZE = 8192


def draw_kernel_hat(key, part):
    index_line = jnp.arange(P_SIZE, dtype=jnp.int32)
    offsets = jnp.where(index_line < N, index_line, index_line - P_SIZE).astype(jnp.float32)
    keep_line = (index_line != N).astype(jnp.float32)
    distance = jnp.sqrt(offsets[:, None] * offsets[:, None] + offsets[None, :] * offsets[None, :])
    decay_len = N / 128.0
    decay = jnp.power(1.0 + distance / decay_len, -3.0)
    log_rough = 1.5 * jax.random.truncated_normal(key, -4.0, 4.0, (P_SIZE, P_SIZE), jnp.float32)
    table = decay * jnp.exp(log_rough) * keep_line[:, None] * keep_line[None, :]
    table = table / jnp.sum(table)
    spectrum = jnp.fft.fft2(table)
    return jnp.stack([jnp.transpose(jnp.real(spectrum)), jnp.transpose(jnp.imag(spectrum))]).astype(jnp.float32)


def steps_of(rng, dims, shards, least, top_value):
    level, own = 1.0, jax.random.fold_in(rng, 6)
    for dim, shards_of in shards:
        steps = jnp.exp(jax.random.uniform(jax.random.fold_in(own, dim), (shards_of,), jnp.float32, least / len(shards), top_value / len(shards)))
        level = level * jnp.repeat(steps, dims[dim] // shards_of).reshape([-1 if axis == dim else 1 for axis in range(len(dims))])
    return level


def setup_inputs(seed: int = 0) -> dict:
    seeds = jax.random.split(jax.random.key(seed), 5)
    return {
        "anchors": jnp.clip(jnp.exp(math.log(5.0) - 3.218876 * jax.random.uniform(seeds[0], (N, N), jnp.float32) ** steps_of(seeds[0], (N, N), ((0, 512),), -0.2, 0.2)), 0.2, 5.0),
        "destinations": jnp.clip(jnp.exp(math.log(5.0) - 3.218876 * jax.random.uniform(seeds[1], (N, N), jnp.float32) ** steps_of(seeds[1], (N, N), ((0, 512),), -0.2, 0.2)), 0.2, 5.0),
        "dest_balance": jnp.clip(jnp.exp(math.log(2.0) - 1.3862944 * jax.random.uniform(seeds[2], (N, N), jnp.float32) ** steps_of(seeds[2], (N, N), ((0, 512),), -0.2, 0.2)), 0.5, 2.0),
        "kernel_hat": draw_kernel_hat(jax.random.fold_in(seeds[4], 71), 0),
    }


def reference(anchors, destinations, dest_balance, kernel_hat):
    half = P_SIZE // 2 + 1
    kernel_half = jnp.transpose(lax.complex(kernel_hat[0, :half, :], kernel_hat[1, :half, :]))
    weighted = dest_balance * destinations
    weighted_hat = jnp.fft.rfft2(jnp.pad(weighted, ((0, N), (0, N))))
    first_sum = jnp.fft.irfft2(jnp.conj(kernel_half) * weighted_hat, s=(P_SIZE, P_SIZE))[:N, :N]
    anchor_balance = 1.0 / first_sum
    supply = anchor_balance * anchors
    supply_hat = jnp.fft.rfft2(jnp.pad(supply, ((0, N), (0, N))))
    second_sum = jnp.fft.irfft2(kernel_half * supply_hat, s=(P_SIZE, P_SIZE))[:N, :N]
    return anchor_balance, 1.0 / second_sum
```

```python
import functools

import jax
import jax.numpy as jnp
import ml_dtypes
import numpy as np
from jax import lax
from jax.experimental import pallas as pl
from jax.experimental.pallas import tpu as pltpu
from jax.sharding import PartitionSpec as P

MESH = pl.DeviceIdType.MESH
F32 = jnp.float32
BF16 = jnp.bfloat16
PAD = 8192
FAR_FIRST = [8] + [v for j in range(7, 0, -1) for v in (j, -j)] + [0]


def slot_devices():
    slot = np.arange(512)
    z, p = slot // 32, slot % 32
    return ((z % 8) * 4 + p // 8) * 16 + ((p % 8) // 2) * 4 + (z // 8) * 2 + p % 2


def phase(left, right, modulus):
    return np.exp(-2j * np.pi * (np.outer(left, right) % modulus) / modulus)


def halves(table):
    table = np.asarray(table, np.float32)
    high = table.astype(ml_dtypes.bfloat16)
    return high, (table - high.astype(np.float32)).astype(ml_dtypes.bfloat16)


def lanes_matrix(small):
    real, imag = small.real, small.imag
    block = np.stack([np.stack([real, imag], 1), np.stack([-imag, real], 1)], 0)
    out = np.zeros((2, 8, 8, 2, 8, 8))
    for freq in range(8):
        out[:, :, freq, :, :, freq] = block
    return out.reshape(128, 128)


def turn_pair(table):
    count = table.shape[0]
    real = np.broadcast_to(table.real, (count, 8, 8)).reshape(count, 64)
    imag = np.broadcast_to(table.imag, (count, 8, 8)).reshape(count, 64)
    t1 = np.concatenate([real, real], 1)
    t2 = np.concatenate([-imag, imag], 1)
    return t1.astype(np.float32), t2.astype(np.float32)


def make_tables():
    dev = slot_devices()
    fine = np.arange(512)
    eight = np.arange(8)
    sets = (eight, eight + 1)
    out = {}
    first = np.zeros((128, 256))
    last = np.zeros((256, 128))
    for half in range(2):
        form = np.zeros((8, 8, 2, 8, 8))
        turn = phase(eight, sets[half], 16)
        for s in range(8):
            form[:, s, 0, s, :] = turn.real
            form[:, s, 1, s, :] = turn.imag
        form = form.reshape(64, 128)
        first[:64, half * 128 : half * 128 + 128] = form
        last[half * 128 : half * 128 + 128, :64] = 2.0 * form.T / (PAD * PAD)
    out["first"] = halves(first)
    out["last"] = halves(last)
    pairs = [turn_pair(phase(fine, sets[half], PAD)[:, None, :]) for half in range(2)]
    out["rowturn"] = [np.concatenate([pairs[0][i], pairs[1][i]], 1) for i in range(2)]
    rows = phase(dev, fine, 512)
    out["rowfwd"] = halves(np.concatenate([rows.real, rows.imag], 1))
    back = rows.conj().T
    out["rowinv"] = halves(
        np.concatenate(
            [
                part[:, block * 128 : block * 128 + 128]
                for block in range(4)
                for part in (back.real, back.imag)
            ],
            1,
        )
    )
    cols = phase(np.arange(1024), dev, 1024)
    out["colfwd"] = halves(np.concatenate([cols.real, cols.imag], 1))
    back = cols.conj().T
    out["colinv"] = halves(
        np.concatenate(
            [
                part[:, block * 512 : block * 512 + 512]
                for block in range(2)
                for part in (back.real, back.imag)
            ],
            1,
        )
    )
    out["colturn"] = turn_pair(phase(np.arange(1024), eight, PAD)[:, :, None])
    for name, mat in (("eightf", phase(eight, eight, 8)), ("eighti", phase(eight, eight, 8).conj())):
        out[name] = halves(lanes_matrix(mat))
    return out


ORDER = ("first", "rowturn", "rowfwd", "colfwd", "colturn", "eightf", "eighti", "colinv", "rowinv", "last")


def split(x):
    high = x.astype(BF16)
    return high, (x - high.astype(F32)).astype(BF16)


def dot(a, b):
    return jnp.dot(a, b, preferred_element_type=F32)


def lane_dot(x, high, low):
    xh, xl = split(x)
    return dot(xh, high) + dot(xl, high) + dot(xh, low)


def swap(x):
    return pltpu.roll(x, 64, 1)


def kernel(anchors, dest, bal, khat, *refs):
    hbm = refs[:20]
    ab_out, db_out = refs[20:22]
    (vanch, vdest, vbal, vk, k4, *vt) = refs[22 : 22 + 5 + 20]
    (ka, kb, kc, sent, got, zb, gz, lsem, ssem, rsem, ksem, all_in) = refs[47:]
    tab = {name: (vt[2 * i], vt[2 * i + 1]) for i, name in enumerate(ORDER)}

    row, col = lax.axis_index("row"), lax.axis_index("col")
    z = (col // 2 % 2) * 8 + row // 4
    p = (row % 4) * 8 + (col // 4) * 2 + col % 2
    me = z * 32 + p

    def device(zz, pp):
        return ((zz % 8) * 4 + pp // 8, ((pp % 8) // 2) * 4 + (zz // 8) * 2 + pp % 2)

    loads = {}

    def load(name, src, dst):
        copy = pltpu.make_async_copy(src, dst, lsem.at[len(loads)])
        loads[name] = copy
        copy.start()

    load("dest", dest, vdest)
    load("bal", bal, vbal)
    for i in range(3 * 2):
        load((ORDER[i // 2], i % 2), hbm[i], vt[i])
    load("khat", khat, vk)
    for i in range(3 * 2, 20):
        load((ORDER[i // 2], i % 2), hbm[i], vt[i])
    load("anchors", anchors, vanch)

    k4[...] = jnp.zeros_like(k4)
    barrier = pltpu.get_barrier_semaphore()

    def greet_z(k, carry):
        pl.semaphore_signal(barrier, inc=1, device_id=device((z + k) % 16, p), device_id_type=MESH)
        return carry

    def greet_p(k, carry):
        pl.semaphore_signal(barrier, inc=1, device_id=device(z, (p + k) % 32), device_id_type=MESH)
        return carry

    lax.fori_loop(1, 16, greet_z, 0)
    lax.fori_loop(1, 32, greet_p, 0)

    lane = lax.broadcasted_iota(jnp.int32, (1, 128), 1)
    freq0 = lane % 8 == 0
    re_lane = lane < 64
    re0 = (freq0 & re_lane).astype(F32)
    im0 = (freq0 & (lane >= 64)).astype(F32)
    alt = 1.0 - 2.0 * (lax.broadcasted_iota(jnp.int32, (512, 128), 0) % 2).astype(F32)
    neg_re = jnp.where(re_lane, -1.0, 1.0).astype(F32)

    def stack_turned(x):
        return jnp.concatenate([x, swap(x) * neg_re], 0)

    def table_dot(refs_, rows, cols, x):
        xh, xl = split(x)
        wide = dot(refs_[0][rows, cols], jnp.concatenate([xh, xl], 1))
        return wide[:, :128] + wide[:, 128:] + dot(refs_[1][rows, cols], xh)

    def rows_forward(v, out):
        blocks = [v[:, 512 * i : 512 * i + 512] for i in range(8)]
        v64 = jnp.concatenate(blocks + [jnp.zeros((64, 512), F32)], 0)
        vt_ = v64.T
        h = lane_dot(vt_, tab["first"][0][...], tab["first"][1][...])
        hs = []
        for half in range(2):
            lanes = slice(half * 128, half * 128 + 128)
            g = h[:, lanes]
            hs.append(g * tab["rowturn"][0][:, lanes] + swap(g) * tab["rowturn"][1][:, lanes])
        nyq = swap(jnp.sum(hs[0] * alt, axis=0, keepdims=True)) * im0
        for half in range(2):
            x = stack_turned(hs[half])
            for part in range(2):
                rows = slice((2 * part + half) * 128, (2 * part + half) * 128 + 128)
                out[rows, :] = table_dot(tab["rowfwd"], rows, slice(None), x)
        out[0:1, :] = out[0:1, :] + nyq

    def rows_inverse(src):
        acc = jnp.zeros((512, 128), F32)
        top = src[0:1, :]
        nyq = swap(top * im0) * 0.5
        for half in range(2):
            g = jnp.zeros((512, 128), F32)
            for part in range(2):
                block = 2 * part + half
                x = src[block * 128 : block * 128 + 128, :]
                if block == 0:
                    keep = 1.0 - 0.5 * re0 - im0
                    first_row = lax.broadcasted_iota(jnp.int32, (128, 128), 0) == 0
                    x = jnp.where(first_row, x * keep, x)
                g = g + table_dot(
                    tab["rowinv"], slice(None), slice(block * 256, block * 256 + 256), stack_turned(x)
                )
            if half == 0:
                g = g + alt * nyq
            lanes = slice(half * 128, half * 128 + 128)
            g = g * tab["rowturn"][0][:, lanes] - swap(g) * tab["rowturn"][1][:, lanes]
            acc = acc + lane_dot(g, tab["last"][0][lanes, :], tab["last"][1][lanes, :])
        y64 = acc.T
        return jnp.concatenate([y64[8 * i : 8 * i + 8, :] for i in range(8)], 1)

    def columns(src, out, turn):
        zb[0] = stack_turned(src[...])

        @pl.when(me == 0)
        def _():
            zb[1] = stack_turned(src[...] * (-neg_re))

        for chunk in range(2):
            rows = slice(chunk * 512, chunk * 512 + 512)
            t1, t2 = tab["colturn"][0][rows, :], tab["colturn"][1][rows, :]

            def spectrum(which):
                g = table_dot(tab["colfwd"], rows, slice(None), zb[which])
                g = g * t1 + swap(g) * t2
                return lane_dot(g, tab["eightf"][0][...], tab["eightf"][1][...])

            y = spectrum(0)
            gz[...] = y * ka[rows, :] + swap(y) * (turn * kb[rows, :])

            @pl.when(me == 0)
            def _():
                yc = spectrum(1)
                kct = kc[rows, :]
                kcs = swap(kct)
                kca = jnp.where(re_lane, kct, kcs)
                kcb = jnp.where(re_lane, -kcs, kct)
                gz[...] = gz[...] + yc * kca + swap(yc) * (turn * kcb)

            g = lane_dot(gz[...], tab["eighti"][0][...], tab["eighti"][1][...])
            g = g * t1 - swap(g) * t2
            part = table_dot(
                tab["colinv"], slice(None), slice(chunk * 1024, chunk * 1024 + 1024), stack_turned(g)
            )
            out[...] = part if chunk == 0 else out[...] + part

    def exchange(step):
        src, dst = sent.at[step], got.at[step]
        for offset in FAR_FIRST:
            zz = (z + offset + 16) % 16

            def send(k, carry):
                pp = (p + k) % 32
                pltpu.make_async_remote_copy(
                    src_ref=src.at[pl.ds(zz * 32 + pp, 1)],
                    dst_ref=dst.at[pl.ds(me, 1)],
                    send_sem=ssem.at[step],
                    recv_sem=rsem.at[step],
                    device_id=device(zz, pp),
                    device_id_type=MESH,
                ).start()
                return carry

            lax.fori_loop(1 if offset == 0 else 0, 32, send, 0, unroll=1 if offset == 0 else 8)
        own = pltpu.make_async_copy(src.at[pl.ds(me, 1)], dst.at[pl.ds(me, 1)], lsem.at[24])
        own.start()
        own.wait()
        everything = pltpu.make_async_remote_copy(
            src_ref=src.at[pl.ds(0, 511)],
            dst_ref=dst.at[pl.ds(0, 511)],
            send_sem=ssem.at[step],
            recv_sem=rsem.at[step],
            device_id=device(z, p),
            device_id_type=MESH,
        )
        everything.wait_send()
        everything.wait_recv()

    for key in ("dest", "bal") + tuple((n, i) for n in ORDER[:3] for i in range(2)):
        loads.pop(key).wait()
    rows_forward(vbal[...] * vdest[...], sent.at[0])

    pl.semaphore_wait(barrier, 46)

    def tell_z(k, carry):
        pl.semaphore_signal(all_in, inc=1, device_id=device((z + k) % 16, p), device_id_type=MESH)
        return carry

    lax.fori_loop(1, 16, tell_z, 0)
    pl.semaphore_wait(all_in, 15)

    exchange_k4(row, col, vk, k4, ksem, loads)
    for key in tuple(loads):
        loads.pop(key).wait()
    exchange(0)

    low = row < 16
    pieces = []
    for c in range(2):
        for m in range(8):
            lanes = slice(m * 1024, m * 1024 + 1024)
            pieces.append(jnp.where(low, vk[c, 0:8, lanes], vk[c, 1:9, lanes]))
    kt = jnp.concatenate(pieces, 0).T
    ks = swap(kt)
    ka[...] = jnp.where(re_lane, kt, ks)
    kb[...] = jnp.where(re_lane, -ks, kt)

    @pl.when(me == 0)
    def _():
        wait_k4(vk, k4, ksem)
        own = jnp.where(re_lane, ka[...], kb[...])
        nyq_pieces = []
        for c in range(2):
            for m in range(8):
                nyq_pieces.append(k4[c, :, m * 1024 : m * 1024 + 1024])
        nyq = jnp.concatenate(nyq_pieces, 0).T
        kc[...] = jnp.where(freq0, 0.5 * (own - nyq), 0.0)
        mean = jnp.where(freq0, 0.5 * (own + nyq), own)
        ms = swap(mean)
        ka[...] = jnp.where(re_lane, mean, ms)
        kb[...] = jnp.where(re_lane, -ms, mean)

    columns(got.at[0], sent.at[1], -1.0)
    exchange(1)
    ab = 1.0 / rows_inverse(got.at[1])
    ab_out[...] = ab
    rows_forward(ab * vanch[...], sent.at[2])
    exchange(2)
    columns(got.at[2], sent.at[3], 1.0)
    exchange(3)
    db_out[...] = 1.0 / rows_inverse(got.at[3])


def k4_copy(vk, k4, ksem, device_id):
    return pltpu.make_async_remote_copy(
        src_ref=vk.at[:, pl.ds(0, 1)],
        dst_ref=k4.at[:, pl.ds(0, 1)],
        send_sem=ksem.at[0],
        recv_sem=ksem.at[1],
        device_id=device_id,
        device_id_type=MESH,
    )


def exchange_k4(row, col, vk, k4, ksem, loads):
    loads.pop("khat").wait()

    @pl.when((row == 16) & (col == 0))
    def _():
        copy = k4_copy(vk, k4, ksem, (row - 16, col))
        copy.start()
        copy.wait_send()


def wait_k4(vk, k4, ksem):
    row, col = lax.axis_index("row"), lax.axis_index("col")
    k4_copy(vk, k4, ksem, (row + 16, col)).wait_recv()


def per_device(anchors, destinations, dest_balance, kernel_hat):
    tables = make_tables()
    consts = [jnp.asarray(t) for name in ORDER for t in tables[name]]
    vmem = pl.BlockSpec(memory_space=pltpu.VMEM)
    anywhere = pl.BlockSpec(memory_space=pl.ANY)
    grid = jax.ShapeDtypeStruct(anchors.shape, F32)
    dma = pltpu.SemaphoreType.DMA
    scratch = [pltpu.VMEM(anchors.shape, F32)] * 3
    scratch += [pltpu.VMEM(kernel_hat.shape, F32), pltpu.VMEM((2, 8, PAD), F32)]
    scratch += [pltpu.VMEM(c.shape, c.dtype) for c in consts]
    scratch += [pltpu.VMEM((1024, 128), F32)] * 3
    scratch += [pltpu.VMEM((4, 512, 128), F32)] * 2
    scratch += [pltpu.VMEM((2, 1024, 128), F32), pltpu.VMEM((512, 128), F32)]
    scratch += [dma((32,)), dma((4,)), dma((4,)), dma((2,)), pltpu.SemaphoreType.REGULAR]
    return pl.pallas_call(
        kernel,
        out_shape=(grid, grid),
        in_specs=[anywhere] * (4 + len(consts)),
        out_specs=(vmem, vmem),
        scratch_shapes=scratch,
        compiler_params=pltpu.CompilerParams(
            collective_id=0, has_side_effects=True, vmem_limit_bytes=56 << 20
        ),
        cost_estimate=pl.CostEstimate(flops=4 << 30, bytes_accessed=20 << 20, transcendentals=0),
    )(anchors, destinations, dest_balance, kernel_hat, *consts)


def solution(mesh):
    rows = P(("row", "col"), None)
    return jax.shard_map(
        per_device,
        mesh=mesh,
        in_specs=(rows, rows, rows, P(None, ("row", "col"), None)),
        out_specs=(rows, rows),
        check_vma=False,
    )
```

```python
import functools

import jax
import jax.numpy as jnp
import ml_dtypes
import numpy as np
from jax import lax
from jax.experimental import pallas as pl
from jax.experimental.pallas import tpu as pltpu
from jax.sharding import PartitionSpec as P

MESH = pl.DeviceIdType.MESH
F32 = jnp.float32
BF16 = jnp.bfloat16
PAD = 8192
TRANSLATIONS = [(i, j, k) for i in (2, 1, 3, 0) for j in (2, 1, 3, 0) for k in (1, 0)]


def slot_devices():
    slot = np.arange(512)
    z, p = slot // 32, slot % 32
    return ((z % 8) * 4 + p // 8) * 16 + ((p % 8) // 2) * 4 + (z // 8) * 2 + p % 2


def phase(left, right, modulus):
    return np.exp(-2j * np.pi * (np.outer(left, right) % modulus) / modulus)


def halves(table):
    table = np.asarray(table, np.float32)
    high = table.astype(ml_dtypes.bfloat16)
    return high, (table - high.astype(np.float32)).astype(ml_dtypes.bfloat16)


def stacked(table):
    high, low = halves(table)
    return np.concatenate([high, high], 0), low


def lanes_matrix(small):
    real, imag = small.real, small.imag
    block = np.stack([np.stack([real, imag], 1), np.stack([-imag, real], 1)], 0)
    out = np.zeros((2, 8, 8, 2, 8, 8))
    for freq in range(8):
        out[:, :, freq, :, :, freq] = block
    return out.reshape(128, 128)


def turn_pair(table):
    count = table.shape[0]
    real = np.broadcast_to(table.real, (count, 8, 8)).reshape(count, 64)
    imag = np.broadcast_to(table.imag, (count, 8, 8)).reshape(count, 64)
    t1 = np.concatenate([real, real], 1)
    t2 = np.concatenate([-imag, imag], 1)
    return t1.astype(np.float32), t2.astype(np.float32)


def make_tables():
    dev = slot_devices()
    fine = np.arange(512)
    eight = np.arange(8)
    sets = (eight, eight + 1)
    out = {}
    first = np.zeros((128, 256))
    last = np.zeros((256, 128))
    for half in range(2):
        form = np.zeros((8, 8, 2, 8, 8))
        turn = phase(eight, sets[half], 16)
        for s in range(8):
            form[:, s, 0, s, :] = turn.real
            form[:, s, 1, s, :] = turn.imag
        form = form.reshape(64, 128)
        first[:64, half * 128 : half * 128 + 128] = form
        last[half * 128 : half * 128 + 128, :64] = 2.0 * form.T / (PAD * PAD)
    out["first"] = stacked(first)
    out["last"] = tuple(
        np.concatenate(pair, 0) for pair in zip(stacked(last[:128]), stacked(last[128:]))
    )
    pairs = [turn_pair(phase(fine, sets[half], PAD)[:, None, :]) for half in range(2)]
    out["rowturn"] = [np.concatenate([pairs[0][i], pairs[1][i]], 1) for i in range(2)]
    even = np.concatenate([np.arange(128), np.arange(256, 384)])
    rows = phase(np.concatenate([dev[even], dev[even + 128]]), fine, 512)
    out["rowfwd"] = halves(np.concatenate([rows.real, rows.imag], 1))
    back = phase(fine, dev, 512).conj()
    out["rowinv"] = halves(
        np.concatenate(
            [
                part[:, block * 128 : block * 128 + 128]
                for block in range(4)
                for part in (back.real, back.imag)
            ],
            1,
        )
    )
    base = dev[even]
    quarter = np.arange(256)
    cols = phase(quarter, base, 256)
    out["colfwd"] = halves(np.concatenate([cols.real, cols.imag], 1))
    back = cols.conj().T
    out["colinv"] = halves(np.concatenate([back.real, back.imag], 1))
    turns = np.concatenate([phase(base, np.array([r]), 1024) for r in range(1, 4)], 0)
    out["devturn"] = turn_pair(turns[:, :, None])
    freqs = (quarter[None, :] * 4 + np.arange(4)[:, None]).reshape(-1)
    out["colturn"] = turn_pair(phase(freqs, eight, PAD)[:, :, None])
    packed = np.where(eight < 4, phase(freqs, eight, PAD).reshape(4, 256, 8, 1)[eight % 4, :, :, 0].transpose(1, 2, 0), 0.0)
    out["packturn"] = turn_pair(packed)
    for name, mat in (("eightf", phase(eight, eight, 8)), ("eighti", phase(eight, eight, 8).conj())):
        out[name] = stacked(lanes_matrix(mat))
    return out


ORDER = (
    "first", "rowturn", "rowfwd", "devturn", "colfwd", "colturn", "packturn", "eightf", "eighti", "colinv", "rowinv", "last",
)
TABLES = 2 * len(ORDER)


def split(x):
    high = x.astype(BF16)
    return high, (x - high.astype(F32)).astype(BF16)


def dot(a, b):
    return jnp.dot(a, b, preferred_element_type=F32)


def lane_dot(x, high, low):
    xh, xl = split(x)
    return dot(jnp.concatenate([xh, xl], 1), high) + dot(xh, low)


def swap(x):
    return pltpu.roll(x, 64, 1)


def kernel(anchors, dest, bal, khat, *refs):
    hbm, refs = refs[:TABLES], refs[TABLES:]
    (factors, vanch, vdest, vbal, vk, k4), refs = refs[:6], refs[6:]
    vt, refs = refs[:TABLES], refs[TABLES:]
    (kt, ka, kb, kc, sent, got, gz, lsem, ssem, rsem, ksem, all_in) = refs
    tab = {name: (vt[2 * i], vt[2 * i + 1]) for i, name in enumerate(ORDER)}

    row, col = lax.axis_index("row"), lax.axis_index("col")
    z = (col // 2 % 2) * 8 + row // 4
    p = (row % 4) * 8 + (col // 4) * 2 + col % 2
    me = z * 32 + p

    xs = [lax.rem(row + i, 4) for i in range(4)]
    ys = [lax.rem(lax.div(col, 4) + i, 4) for i in range(4)]
    cores = [lax.rem(col, 2), 1 - lax.rem(col, 2)]

    def z_base(zz):
        return lax.rem(zz, 8) * 4, lax.div(zz, 8) * 2

    def z_device(offset):
        first_row, first_col = z_base(lax.rem(z + offset, 16))
        return first_row + xs[0], first_col + (ys[0] * 4 + cores[0])

    loads = {}

    def load(name, src, dst):
        copy = pltpu.make_async_copy(src, dst, lsem.at[len(loads)])
        loads[name] = copy
        copy.start()

    load("dest", dest, vdest)
    load("bal", bal, vbal)
    for i in range(3 * 2):
        load((ORDER[i // 2], i % 2), hbm[i], vt[i])
    k4[...] = jnp.zeros_like(k4)
    barrier = pltpu.get_barrier_semaphore()

    for offset in range(1, 16):
        pl.semaphore_signal(barrier, inc=1, device_id=z_device(offset), device_id_type=MESH)
    own_row, own_col = z_base(z)
    for i, j, k in TRANSLATIONS[:-1]:
        target = (own_row + xs[i], own_col + (ys[j] * 4 + cores[k]))
        pl.semaphore_signal(barrier, inc=1, device_id=target, device_id_type=MESH)

    load("khat", khat, vk)
    for i in range(3 * 2, TABLES):
        load((ORDER[i // 2], i % 2), hbm[i], vt[i])
    load("anchors", anchors, vanch)

    lane = lax.broadcasted_iota(jnp.int32, (1, 128), 1)
    freq0 = lane % 8 == 0
    re_lane = lane < 64
    re0 = (freq0 & re_lane).astype(F32)
    im0 = (freq0 & (lane >= 64)).astype(F32)
    alt = 1.0 - 2.0 * (lax.broadcasted_iota(jnp.int32, (512, 128), 0) % 2).astype(F32)
    neg_re = jnp.where(re_lane, -1.0, 1.0).astype(F32)

    def times_i(x):
        return swap(x) * neg_re

    def stack_turned(x):
        return jnp.concatenate([x, times_i(x)], 0)

    def table_dot(refs_, rows, cols, x):
        xh, xl = split(x)
        wide = dot(refs_[0][rows, cols], jnp.concatenate([xh, xl], 1))
        return wide[:, :128] + wide[:, 128:] + dot(refs_[1][rows, cols], xh)

    def rows_forward(v, out):
        blocks = [v[:, 512 * i : 512 * i + 512] for i in range(8)]
        v64 = jnp.concatenate(blocks + [jnp.zeros((64, 512), F32)], 0)
        vt_ = v64.T
        h = lane_dot(vt_, tab["first"][0][...], tab["first"][1][...])
        hs = []
        for half in range(2):
            lanes = slice(half * 128, half * 128 + 128)
            g = h[:, lanes]
            hs.append(g * tab["rowturn"][0][:, lanes] + swap(g) * tab["rowturn"][1][:, lanes])
        nyq = swap(jnp.sum(hs[0] * alt, axis=0, keepdims=True)) * im0
        for half in range(2):
            x = stack_turned(hs[half])
            y = table_dot(tab["rowfwd"], slice(256 * half, 256 * half + 256), slice(None), x)
            out[128 * half : 128 * half + 128, :] = y[:128]
            out[128 * half + 256 : 128 * half + 384, :] = y[128:]
        out[0:1, :] = out[0:1, :] + nyq

    def rows_inverse(src):
        acc = jnp.zeros((512, 128), F32)
        top = src[0:1, :]
        nyq = swap(top * im0) * 0.5
        for half in range(2):
            g = jnp.zeros((512, 128), F32)
            for part in range(2):
                block = 2 * part + half
                x = src[block * 128 : block * 128 + 128, :]
                if block == 0:
                    keep = 1.0 - 0.5 * re0 - im0
                    first_row = lax.broadcasted_iota(jnp.int32, (128, 128), 0) == 0
                    x = jnp.where(first_row, x * keep, x)
                g = g + table_dot(
                    tab["rowinv"], slice(None), slice(block * 256, block * 256 + 256), stack_turned(x)
                )
            if half == 0:
                g = g + alt * nyq
            lanes = slice(half * 128, half * 128 + 128)
            g = g * tab["rowturn"][0][:, lanes] - swap(g) * tab["rowturn"][1][:, lanes]
            acc = acc + lane_dot(
                g, tab["last"][0][256 * half : 256 * half + 256, :], tab["last"][1][lanes, :]
            )
        y64 = acc.T
        return jnp.concatenate([y64[8 * i : 8 * i + 8, :] for i in range(8)], 1)

    def dev_turn(x, r, sign):
        rows = slice(256 * r - 256, 256 * r)
        return x * tab["devturn"][0][rows, :] + swap(x) * (sign * tab["devturn"][1][rows, :])

    def pack(parts):
        kept = [jnp.where(freq0, part, 0.0) for part in parts]
        return kept[0] + pltpu.roll(kept[1], 1, 1) + pltpu.roll(kept[2], 2, 1) + pltpu.roll(kept[3], 3, 1)

    def columns(src, out, turn):
        def folded(r, flip):
            a = jnp.concatenate([src[0:128, :], src[256:384, :]], 0) * flip
            b = jnp.concatenate([src[128:256, :], src[384:512, :]], 0) * flip
            if r % 2:
                b = times_i(b)
            u = a + b if r in (0, 3) else a - b
            return dev_turn(u, r, 1.0) if r else u

        def spectrum(u, turns, rows):
            g = table_dot(tab["colfwd"], slice(None), slice(None), stack_turned(u))
            g = g * turns[0][rows, :] + swap(g) * turns[1][rows, :]
            return lane_dot(g, tab["eightf"][0][...], tab["eightf"][1][...])

        for r in range(4):
            rows = slice(256 * r, 256 * r + 256)
            y = spectrum(folded(r, 1.0), tab["colturn"], rows)
            gz[rows, :] = y * ka[rows, :] + swap(y) * (turn * kb[rows, :])

        @pl.when(me == 0)
        def _():
            u = pack([folded(r, -neg_re) for r in range(4)])
            yc = spectrum(u, tab["packturn"], slice(None))
            kct = kc[...]
            kcs = swap(kct)
            kca = jnp.where(re_lane, kct, kcs)
            kcb = jnp.where(re_lane, -kcs, kct)
            more = yc * kca + swap(yc) * (turn * kcb)
            for r in range(4):
                rows = slice(256 * r, 256 * r + 256)
                part = pltpu.roll(more, 128 - r, 1) if r else more
                gz[rows, :] = gz[rows, :] + jnp.where(freq0, part, 0.0)

        upper, lower = [], []
        for r in range(4):
            rows = slice(256 * r, 256 * r + 256)
            g = lane_dot(gz[rows, :], tab["eighti"][0][...], tab["eighti"][1][...])
            g = g * tab["colturn"][0][rows, :] - swap(g) * tab["colturn"][1][rows, :]
            v = table_dot(tab["colinv"], slice(None), slice(None), stack_turned(g))
            if r:
                v = dev_turn(v, r, -1.0)
            upper.append(v)
            lower.append(times_i(v) if r % 2 else v)
        first = (upper[0] + upper[2]) + (upper[1] + upper[3])
        second = (lower[0] - lower[2]) + (lower[1] - lower[3])
        out[0:128, :] = first[:128]
        out[128:256, :] = second[:128]
        out[256:384, :] = first[128:]
        out[384:512, :] = second[128:]

    def send_group(step, zz, moves):
        first_row, first_col = z_base(zz)
        first_slot = zz * 32
        for i, j, k in moves:
            slot = first_slot + (xs[i] * 8 + ys[j] * 2 + cores[k])
            pltpu.make_async_remote_copy(
                src_ref=sent.at[step, pl.ds(slot, 1)],
                dst_ref=got.at[step, pl.ds(me, 1)],
                send_sem=ssem.at[step],
                recv_sem=rsem.at[step],
                device_id=(first_row + xs[i], first_col + (ys[j] * 4 + cores[k])),
                device_id_type=MESH,
            ).start()

    def send_plane(step):
        send_group(step, z, TRANSLATIONS[:-1])

    def send_far(step):
        def one(i, carry):
            distance = 8 - (i + 1) // 2
            offset = jnp.where(i % 2 == 1, distance, 16 - distance)
            send_group(step, lax.rem(z + offset, 16), TRANSLATIONS)
            return carry

        lax.fori_loop(0, 15, one, 0)

    def exchange_wait(step):
        src, dst = sent.at[step], got.at[step]
        own = pltpu.make_async_copy(src.at[pl.ds(me, 1)], dst.at[pl.ds(me, 1)], lsem.at[31])
        own.start()
        own.wait()
        everything = pltpu.make_async_remote_copy(
            src_ref=src.at[pl.ds(0, 511)],
            dst_ref=dst.at[pl.ds(0, 511)],
            send_sem=ssem.at[step],
            recv_sem=rsem.at[step],
            device_id=z_device(0),
            device_id_type=MESH,
        )
        everything.wait_send()
        everything.wait_recv()

    for key in ("dest", "bal") + tuple((n, i) for n in ORDER[:3] for i in range(2)):
        loads.pop(key).wait()
    rows_forward(vbal[...] * vdest[...], sent.at[0])

    pl.semaphore_wait(barrier, 46)

    for offset in range(1, 16):
        pl.semaphore_signal(all_in, inc=1, device_id=z_device(offset), device_id_type=MESH)

    exchange_k4(row, col, vk, k4, ksem, loads)
    send_plane(0)
    pl.semaphore_wait(all_in, 15)

    low = row < 16

    def own_piece(c, lanes):
        return jnp.where(low, vk[c, 0:8, lanes], vk[c, 1:9, lanes])

    def nyq_piece(c, lanes):
        return k4[c, :, lanes]

    def turn_rows(piece, j):
        lanes = [slice(m * 1024 + j * 128, m * 1024 + j * 128 + 128) for m in range(8)]
        kt[128 * j : 128 * j + 128, :] = jnp.concatenate(
            [piece(c, lanes[m]) for c in range(2) for m in range(8)], 0
        ).T

    def residue(r):
        return kt[pl.ds(r, 256, stride=4), :]

    def store_spectrum(r, spec):
        rows = slice(256 * r, 256 * r + 256)
        turned = swap(spec)
        ka[rows, :] = jnp.where(re_lane, spec, turned)
        kb[rows, :] = jnp.where(re_lane, -turned, spec)

    steps = [functools.partial(turn_rows, own_piece, j) for j in range(8)]
    steps += [lambda r=r: store_spectrum(r, residue(r)) for r in range(4)]

    def finish_loads():
        for key in tuple(loads):
            loads.pop(key).wait()

    send_far(0)
    for piece in steps + [finish_loads]:
        piece()

    @pl.when(me == 0)
    def _():
        wait_k4(vk, k4, ksem)
        for j in range(8):
            turn_rows(nyq_piece, j)
        apart = []
        for r in range(4):
            rows = slice(256 * r, 256 * r + 256)
            own = jnp.where(re_lane, ka[rows, :], kb[rows, :])
            nyq = residue(r)
            apart.append(0.5 * (own - nyq))
            store_spectrum(r, jnp.where(freq0, 0.5 * (own + nyq), own))
        kc[...] = pack(apart)

    exchange_wait(0)
    columns(got.at[0], sent.at[1], -1.0)
    send_far(1)
    send_plane(1)
    exchange_wait(1)
    ab = 1.0 / rows_inverse(got.at[1])
    factors[0:8, :] = ab
    rows_forward(ab * vanch[...], sent.at[2])
    send_far(2)
    send_plane(2)
    exchange_wait(2)
    columns(got.at[2], sent.at[3], 1.0)
    send_far(3)
    send_plane(3)
    exchange_wait(3)
    factors[8:16, :] = 1.0 / rows_inverse(got.at[3])


def k4_copy(vk, k4, ksem, device_id):
    return pltpu.make_async_remote_copy(
        src_ref=vk.at[:, pl.ds(0, 1)],
        dst_ref=k4.at[:, pl.ds(0, 1)],
        send_sem=ksem.at[0],
        recv_sem=ksem.at[1],
        device_id=device_id,
        device_id_type=MESH,
    )


def exchange_k4(row, col, vk, k4, ksem, loads):
    loads.pop("khat").wait()

    @pl.when((row == 16) & (col == 0))
    def _():
        copy = k4_copy(vk, k4, ksem, (row - 16, col))
        copy.start()
        copy.wait_send()


def wait_k4(vk, k4, ksem):
    row, col = lax.axis_index("row"), lax.axis_index("col")
    k4_copy(vk, k4, ksem, (row + 16, col)).wait_recv()


def per_device(anchors, destinations, dest_balance, kernel_hat):
    tables = make_tables()
    consts = [jnp.asarray(t) for name in ORDER for t in tables[name]]
    vmem = pl.BlockSpec(memory_space=pltpu.VMEM)
    anywhere = pl.BlockSpec(memory_space=pl.ANY)
    count, width = anchors.shape
    dma = pltpu.SemaphoreType.DMA
    scratch = [pltpu.VMEM(anchors.shape, F32)] * 3
    scratch += [pltpu.VMEM(kernel_hat.shape, F32), pltpu.VMEM((2, 8, PAD), F32)]
    scratch += [pltpu.VMEM(c.shape, c.dtype) for c in consts]
    scratch += [pltpu.VMEM((1024, 128), F32)] * 3 + [pltpu.VMEM((256, 128), F32)]
    scratch += [pltpu.VMEM((4, 512, 128), F32)] * 2
    scratch += [pltpu.VMEM((1024, 128), F32)]
    scratch += [dma((32,)), dma((4,)), dma((4,)), dma((2,)), pltpu.SemaphoreType.REGULAR]
    factors = pl.pallas_call(
        kernel,
        out_shape=jax.ShapeDtypeStruct((2 * count, width), F32),
        in_specs=[anywhere] * (4 + len(consts)),
        out_specs=vmem,
        scratch_shapes=scratch,
        compiler_params=pltpu.CompilerParams(
            collective_id=0, has_side_effects=True, vmem_limit_bytes=56 << 20
        ),
        cost_estimate=pl.CostEstimate(flops=4 << 30, bytes_accessed=20 << 20, transcendentals=0),
    )(anchors, destinations, dest_balance, kernel_hat, *consts)
    return factors[:count], factors[count:]


def solution(mesh):
    rows = P(("row", "col"), None)
    return jax.shard_map(
        per_device,
        mesh=mesh,
        in_specs=(rows, rows, rows, P(None, ("row", "col"), None)),
        out_specs=(rows, rows),
        check_vma=False,
    )
```
